32 devices in a mesh: groups: 2 (over y), rows: 4 (over z), disp: 2 (over x), cols: 2 (over core).
Axes of the slice: x: 2, y: 2, z: 4, core: 2. Of those that a mesh axis runs over, the one named last changes fastest.
Arguments:
- cost_volume_section: bfloat16 [32, 32, 8192], P(('groups', 'rows'), 'cols', 'disp'), parts along dimension 0, may hold values from -6 to 6
- picture_convolution_taps_grid: bfloat16 [3, 3, 3, 64, 64], replicated, may hold values from -0.25 to 0.25
- picture_convolution_offset_terms: float32 [3, 64], replicated, may hold values from -3 to 3
- shiftaxis_convolution_taps: bfloat16 [2, 17, 64, 64], replicated, may hold values from -0.1875 to 0.1875
- shiftaxis_convolution_biases: float32 [2, 64], replicated, may hold values from -3 to 3
- prior_norm_scale: float32 [64], replicated, may hold values from 0.1 to 1.9
- qkv_side_projections: bfloat16 [64, 192], replicated, may hold values from -0.75 to 0.75
- attn_exit_projection: bfloat16 [64, 64], replicated, may hold values from -0.75 to 0.75
- each_mixer_scale: float32 [4], replicated, may hold values from 0.25 to 25, as said below
- gating_projection: bfloat16 [64, 64], replicated, may hold values from -0.75 to 0.75
- gating_offset_terms: float32 [64], replicated, may hold values from -3 to 3
Outputs:
- filtered: bfloat16 [32, 32, 8192], P(('groups', 'rows'), 'cols', 'disp'), parts along dimension 0
The draws below stay inside these ranges and needn't reach their ends.
There are 2 independent parts, one for each index of `groups`. The reference program is written for one: setup_inputs(seed, part) draws one part's arguments, and reference() takes and returns one part's arrays. A program takes and returns all parts, laid end to end along the dimension named above; an argument that names none is the same for every part. Nothing has to cross between parts.
Inputs may be any that keep to these rules, and one draw needn't show every extreme that they name: `each_mixer_scale`: positive score scales, one for each head.
All inputs are finite; a program needn't handle non-finite values.
Results may differ from the reference program's by a relative error of at most 0.0095.
Values may be sent and summed in bfloat16 or wider, within the bound.
A program may use at most 64 MiB of HBM per device.

```python
import math
import jax
import jax.numpy as jnp
from jax import lax

FEATURE_DEPTH = 64
DSP = 128
HEADS = 4
TAPS = 17
FLAT_LAYER_COUNT = 3
H = 16
W = 32


def draw_each_mixer_scale(key, part):
    upper = math.log(8.0)
    uniform_part = jax.random.uniform(key, (HEADS,), jnp.float32)
    return jnp.exp(uniform_part * upper).astype(jnp.float32)


def block_scale(stream_key, dims, pieces, low, top_value):
    def one(axis_at, shards_of):
        steps = jax.random.uniform(jax.random.fold_in(jax.random.fold_in(stream_key, 6), axis_at), (shards_of,), jnp.float32, low / len(pieces), top_value / len(pieces))
        return jnp.repeat(jnp.exp(steps), dims[axis_at] // shards_of).reshape((-1,) + (1,) * (len(dims) - axis_at - 1))

    loudness = one(*pieces[0])
    for cut in pieces[1:]:
        loudness = loudness * one(*cut)
    return loudness


def noise(rng, shape, deviation, most, pieces=(), held_as=jnp.bfloat16):
    result = jax.random.normal(rng, shape, jnp.float32) * deviation
    if len(pieces) > 0:
        result = block_scale(rng, shape, pieces, -0.22, 0.18) * result
    return jnp.clip(result, min=-most, max=most).astype(held_as)


def setup_inputs(seed: int = 0, part: int = 0) -> dict:
    keys = jax.random.split(jax.random.key(seed), 12)
    part_keys = jax.random.split(jax.random.fold_in(keys[11], part), 12)
    return {
        "cost_volume_section": noise(part_keys[0], (H, W, DSP * FEATURE_DEPTH), 1.0, 6.0, ((0, 4), (1, 2), (2, 2))),
        "picture_convolution_taps_grid": noise(keys[1], (FLAT_LAYER_COUNT, 3, 3, FEATURE_DEPTH, FEATURE_DEPTH), (9 * FEATURE_DEPTH) ** -0.5, 0.25),
        "picture_convolution_offset_terms": noise(keys[2], (FLAT_LAYER_COUNT, FEATURE_DEPTH), 0.5, 3.0, (), jnp.float32),
        "shiftaxis_convolution_taps": noise(keys[3], (2, TAPS, FEATURE_DEPTH, FEATURE_DEPTH), (TAPS * FEATURE_DEPTH) ** -0.5, 0.1875),
        "shiftaxis_convolution_biases": noise(keys[4], (2, FEATURE_DEPTH), 0.5, 3.0, (), jnp.float32),
        "prior_norm_scale": jnp.clip(1.0 + 0.18 * jax.random.normal(keys[5], (FEATURE_DEPTH,), jnp.float32), 0.1, 1.9),
        "qkv_side_projections": noise(keys[6], (FEATURE_DEPTH, 3 * FEATURE_DEPTH), FEATURE_DEPTH ** -0.5, 0.75),
        "attn_exit_projection": noise(keys[7], (FEATURE_DEPTH, FEATURE_DEPTH), FEATURE_DEPTH ** -0.5, 0.75),
        "each_mixer_scale": draw_each_mixer_scale(jax.random.fold_in(keys[11], 71), part),
        "gating_projection": noise(keys[9], (FEATURE_DEPTH, FEATURE_DEPTH), FEATURE_DEPTH ** -0.5, 0.75),
        "gating_offset_terms": noise(keys[10], (FEATURE_DEPTH,), 0.5, 3.0, (), jnp.float32),
    }


def image_plane_step(slices_list, kernel, bias_terms):
    border_extended = jnp.pad(slices_list, ((1, 1), (1, 1), (0, 0), (0, 0)))
    row_count = slices_list.shape[0]
    column_count = slices_list.shape[1]
    summed = jnp.zeros(slices_list.shape, jnp.float32)
    for row_tap in range(3):
        for col_tap in range(3):
            window = border_extended[row_tap:row_tap + row_count, col_tap:col_tap + column_count].astype(jnp.float32)
            summed = summed + jnp.einsum('rwdc,co->rwdo', window, kernel[row_tap, col_tap].astype(jnp.float32))
    return jax.nn.silu(summed + bias_terms).astype(jnp.bfloat16)

def parallax_step(image_lines, kernel, bias_terms):
    tap_count = kernel.shape[0]
    half_span = tap_count // 2
    candidate_levels = image_lines.shape[1]
    border_extended = jnp.pad(image_lines, ((0, 0), (half_span, half_span), (0, 0))).astype(jnp.float32)
    summed = jnp.zeros(image_lines.shape, jnp.float32)
    for tap_index in range(tap_count):
        window = border_extended[:, tap_index:tap_index + candidate_levels]
        summed = summed + jnp.einsum('pdc,co->pdo', window, kernel[tap_index].astype(jnp.float32))
    return summed + bias_terms

def project(latter_result, prior_norm_scale, qkv_side_projections):
    wide_copy = latter_result.astype(jnp.float32)
    normed = (wide_copy * lax.rsqrt(lax.optimization_barrier(jnp.mean(wide_copy * wide_copy, axis=-1, keepdims=True)) + 1e-05) * prior_norm_scale).astype(jnp.bfloat16)
    joined = jnp.einsum('pdc,ce->pde', normed.astype(jnp.float32), qkv_side_projections.astype(jnp.float32)).astype(jnp.bfloat16)
    feat_width = latter_result.shape[-1]
    return (joined[..., :feat_width], joined[..., feat_width:2 * feat_width], joined[..., 2 * feat_width:])

def displacement_self_mixing(probe_items, address_items, payload_items, each_mixer_scale):
    pixel_count, candidate_levels, feat_width = probe_items.shape
    arm_index = each_mixer_scale.shape[0]
    lanes_each = feat_width // arm_index
    query_heads = probe_items.astype(jnp.float32).reshape(pixel_count, candidate_levels, arm_index, lanes_each)
    key_heads = address_items.astype(jnp.float32).reshape(pixel_count, -1, arm_index, lanes_each)
    value_heads = payload_items.astype(jnp.float32).reshape(pixel_count, -1, arm_index, lanes_each)
    softmax_scale_amount = each_mixer_scale / math.sqrt(lanes_each)
    scores = jnp.einsum('pqhc,pkhc->phqk', query_heads, key_heads) * softmax_scale_amount[None, :, None, None]
    soft_weights = jax.nn.softmax(scores, axis=-1).astype(jnp.bfloat16)
    reunited_arms = jnp.einsum('phqk,pkhc->pqhc', soft_weights.astype(jnp.float32), value_heads)
    return reunited_arms.reshape(pixel_count, candidate_levels, feat_width).astype(jnp.bfloat16)

def finish(latter_result, reunited_arms, attn_exit_projection):
    moved = jnp.einsum('pdc,ce->pde', reunited_arms.astype(jnp.float32), attn_exit_projection.astype(jnp.float32))
    return (latter_result.astype(jnp.float32) + moved).astype(jnp.bfloat16)

def reference(cost_volume_section, picture_convolution_taps_grid, picture_convolution_offset_terms, shiftaxis_convolution_taps, shiftaxis_convolution_biases, prior_norm_scale, qkv_side_projections, attn_exit_projection, each_mixer_scale, gating_projection, gating_offset_terms):
    height = cost_volume_section.shape[0]
    column_count = cost_volume_section.shape[1]
    slices_list = cost_volume_section.reshape(height, column_count, DSP, FEATURE_DEPTH)
    for level_ordinal in range(FLAT_LAYER_COUNT):
        slices_list = image_plane_step(slices_list, picture_convolution_taps_grid[level_ordinal], picture_convolution_offset_terms[level_ordinal])

    def one_row(row_pair):
        horizontal_line, volume_row = row_pair
        initial_result = jax.nn.silu(parallax_step(horizontal_line, shiftaxis_convolution_taps[0], shiftaxis_convolution_biases[0])).astype(jnp.bfloat16)
        latter_result = parallax_step(initial_result, shiftaxis_convolution_taps[1], shiftaxis_convolution_biases[1]).astype(jnp.bfloat16)
        probe_items, address_items, payload_items = project(latter_result, prior_norm_scale, qkv_side_projections)
        reunited_arms = displacement_self_mixing(probe_items, address_items, payload_items, each_mixer_scale)
        attended = finish(latter_result, reunited_arms, attn_exit_projection)
        gate_value = jax.nn.sigmoid(jnp.einsum('pdc,ce->pde', attended.astype(jnp.float32), gating_projection.astype(jnp.float32)) + gating_offset_terms)
        gated = volume_row.reshape(column_count, DSP, FEATURE_DEPTH).astype(jnp.float32) * gate_value
        return gated.astype(jnp.bfloat16).reshape(column_count, DSP * FEATURE_DEPTH)
    return lax.map(one_row, (slices_list, cost_volume_section))
```

```python
import functools
import math

import jax
import jax.numpy as jnp
from jax import lax
from jax.experimental import pallas as pl
from jax.experimental.pallas import tpu as pltpu
from jax.sharding import PartitionSpec as P

MESH = pl.DeviceIdType.MESH
BF16 = jnp.bfloat16
F32 = jnp.float32
LANES = 256
DIRECTIONS = [(dy, dx) for dy in (-1, 0, 1) for dx in (-1, 0, 1) if (dy, dx) != (0, 0)]


def sigmoid(v):
    return 0.5 * jnp.tanh(0.5 * v) + 0.5


def dot(a, b):
    return jnp.dot(a, b, preferred_element_type=F32)


def kernel(
    sizes,
    x_ref,
    plane_taps,
    plane_bias,
    shift_taps,
    shift_bias,
    gain_ref,
    qkv_ref,
    exit_ref,
    scale_ref,
    gate_ref,
    gate_bias,
    out_ref,
    fields,
    slabs,
    lines,
    padded,
    second,
    joined,
    mixed,
    back,
    returned,
    stage,
    w_plane,
    w_shift,
    w_qkv,
    w_exit,
    w_gate,
    halo_send,
    halo_recv,
    there_send,
    there_recv,
    back_send,
    back_recv,
):
    nr, nd, nc, H, W, bl, C, layers, taps, heads = sizes
    pack = LANES // C
    B = nd * bl
    half = taps // 2
    reach = (half + pack - 1) // pack
    hr = H // nd
    px = hr * W
    row, disp, col = lax.axis_index("rows"), lax.axis_index("disp"), lax.axis_index("cols")

    def exists(dy, dx):
        ok = None
        for d, at, n in ((dy, row, nr), (dx, col, nc)):
            if d == -1:
                c = at > 0
            elif d == 1:
                c = at < n - 1
            else:
                continue
            ok = c if ok is None else jnp.logical_and(ok, c)
        return ok

    barrier = pltpu.get_barrier_semaphore()
    expected = jnp.int32(nd - 1)
    for dy, dx in DIRECTIONS:
        here = exists(dy, dx)
        expected = expected + here.astype(jnp.int32)

        @pl.when(here)
        def _():
            pl.semaphore_signal(
                barrier, inc=1, device_id={"rows": row + dy, "cols": col + dx}, device_id_type=MESH
            )

    for o in range(1, nd):
        pl.semaphore_signal(
            barrier, inc=1, device_id={"disp": lax.rem(disp + o, nd)}, device_id_type=MESH
        )

    for h in range(H):
        for b in range(bl):
            block = x_ref[h, :, b * LANES : (b + 1) * LANES].astype(F32)
            for s in range(2):
                stage[s, h * bl * W + b * W : h * bl * W + (b + 1) * W, :] = block[
                    :, s * 128 : (s + 1) * 128
                ]
    for h in range(H):
        for w in range(W):
            for s in range(2):
                fields[0, 1 + h, 1 + w, :, s * 128 : (s + 1) * 128] = stage[
                    s, pl.ds(h * bl * W + w, bl, stride=W), :
                ].astype(BF16)

    pl.semaphore_wait(barrier, expected)

    def span(d, n):
        return slice(1, n + 1) if d == 0 else (slice(1, 2) if d == -1 else slice(n, n + 1))

    def landing(d, n):
        return slice(1, n + 1) if d == 0 else (slice(n + 1, n + 2) if d == -1 else slice(0, 1))

    def halo_copy(k, i):
        dy, dx = DIRECTIONS[i]
        return pltpu.make_async_remote_copy(
            src_ref=fields.at[k, span(dy, H), span(dx, W)],
            dst_ref=fields.at[k, landing(dy, H), landing(dx, W)],
            send_sem=halo_send.at[k, i],
            recv_sem=halo_recv.at[k, i],
            device_id={"rows": row + dy, "cols": col + dx},
            device_id_type=MESH,
        )

    order = sorted(range(8), key=lambda i: DIRECTIONS[i][1] != 0)

    def halo_start(k):
        for i in order:
            @pl.when(exists(*DIRECTIONS[i]))
            def _():
                halo_copy(k, i).start()

    def halo_wait(k, which):
        for i in which:
            dy, dx = DIRECTIONS[i]

            @pl.when(exists(-dy, -dx))
            def _():
                halo_copy(k, i).wait_recv()

    halo_start(0)

    for i in range(8):
        dy, dx = DIRECTIONS[i]

        @pl.when(jnp.logical_not(exists(-dy, -dx)))
        def _():
            for k in range(layers):
                view = fields.at[k, landing(dy, H), landing(dx, W)]
                view[...] = jnp.zeros(view.shape, BF16)

    r_at = lax.broadcasted_iota(jnp.int32, (C, LANES), 0)
    l_at = lax.broadcasted_iota(jnp.int32, (C, LANES), 1)
    repeat = (l_at % C == r_at).astype(BF16)
    group = l_at // C

    def spread(w):
        return dot(w, repeat)

    for l in range(layers):
        for t in range(9):
            wide = spread(plane_taps[(l * 9 + t) * C : (l * 9 + t + 1) * C, :])
            for i in range(pack):
                at = t * LANES + i * C
                w_plane[l, at : at + C, :] = jnp.where(group == i, wide, 0.0).astype(BF16)

    bias_p = jnp.concatenate([plane_bias[...]] * pack, axis=1)
    bias_s = jnp.concatenate([shift_bias[...]] * pack, axis=1)
    bias_g = jnp.concatenate([gate_bias[...]] * pack, axis=1)
    gain = jnp.concatenate([gain_ref[...]] * pack, axis=1)

    def late_weights():
        for l in range(2):
            wides = [
                spread(shift_taps[(l * taps + t) * C : (l * taps + t + 1) * C, :])
                for t in range(taps)
            ]
            for j in range(-reach, reach + 1):
                for i in range(pack):
                    value = jnp.zeros((C, LANES), F32)
                    for o in range(pack):
                        t = pack * j + i - o + half
                        if 0 <= t < taps:
                            value = jnp.where(group == o, wides[t], value)
                    at = (j + reach) * LANES + i * C
                    w_shift[l, at : at + C, :] = value.astype(BF16)
        a = lax.broadcasted_iota(jnp.int32, (3 * C, 3 * 128), 0)
        b = lax.broadcasted_iota(jnp.int32, (3 * C, 3 * 128), 1)
        place = jnp.logical_and(a // C == b // 128, a % C == b % 128).astype(BF16)
        wide = dot(qkv_ref[...], place).astype(BF16)
        w_qkv[...] = jnp.zeros(w_qkv.shape, BF16)
        for i in range(pack):
            w_qkv[i * C : (i + 1) * C, i * 384 : (i + 1) * 384] = wide
        w_exit[...] = jnp.zeros(w_exit.shape, BF16)
        wide = spread(exit_ref[...])
        for i in range(pack):
            w_exit[i * 128 : i * 128 + C, :] = jnp.where(group == i, wide, 0.0).astype(BF16)
        wide = spread(gate_ref[...])
        for i in range(pack):
            w_gate[i * C : (i + 1) * C, :] = jnp.where(group == i, wide, 0.0).astype(BF16)
        padded[:, 0:8, :] = jnp.zeros((px, 8, LANES), F32)
        padded[:, B + 8 : B + 16, :] = jnp.zeros((px, 8, LANES), F32)

    def there_copy(o):
        to = lax.rem(disp + o, nd)
        return pltpu.make_async_remote_copy(
            src_ref=slabs.at[to],
            dst_ref=lines.at[disp],
            send_sem=there_send.at[o - 1],
            recv_sem=there_recv.at[o - 1],
            device_id={"disp": to},
            device_id_type=MESH,
        )

    def plane_row(k, h):
        lhs = jnp.concatenate(
            [
                fields[k, h + dy, dx : dx + W].reshape(W * bl, LANES)
                for dy in range(3)
                for dx in range(3)
            ],
            axis=1,
        )
        v = dot(lhs, w_plane[k]) + bias_p[k : k + 1]
        v = (v * sigmoid(v)).astype(BF16).reshape(W, bl, LANES)
        if k + 1 < layers:
            fields[k + 1, 1 + h, 1 : W + 1] = v
        else:
            slabs[h // hr, (h % hr) * W : (h % hr + 1) * W] = v

    sides = [i for i in range(8) if DIRECTIONS[i][0] == 0]
    others = [i for i in range(8) if DIRECTIONS[i][0] != 0]
    for k in range(layers):
        halo_wait(k, sides)
        for h in range(1, H - 1):
            plane_row(k, h)
        if k == 0:
            late_weights()
        halo_wait(k, others)
        for h in (0, H - 1):
            plane_row(k, h)
        if k + 1 < layers:
            halo_start(k + 1)

    for o in range(1, nd):
        there_copy(o).start()
    lines[disp] = slabs[disp]
    for o in range(1, nd):
        there_copy(o).wait_recv()

    for s in range(nd):
        padded[:, 8 + s * bl : 8 + (s + 1) * bl, :] = lines[s].astype(F32)
    step = 8 if px % 8 == 0 else px

    def shift_conv(l, p0):
        lhs = jnp.concatenate(
            [
                padded[pl.ds(p0, step), 8 + j : 8 + j + B, :].astype(BF16).reshape(step * B, LANES)
                for j in range(-reach, reach + 1)
            ],
            axis=1,
        )
        return dot(lhs, w_shift[l]) + bias_s[l : l + 1]

    ones_a = lax.broadcasted_iota(jnp.int32, (LANES, LANES), 0) // C
    ones_b = lax.broadcasted_iota(jnp.int32, (LANES, LANES), 1) // C
    ones = (ones_a == ones_b).astype(BF16)

    def conv_chunk(c, carry):
        p0 = c * step
        v = shift_conv(0, p0)
        v = (v * sigmoid(v)).astype(BF16).astype(F32)
        padded[pl.ds(p0, step), 8 : 8 + B, :] = v.reshape(step, B, LANES)
        v = shift_conv(1, p0).astype(BF16)
        second[pl.ds(p0, step)] = v.reshape(step, B, LANES)
        v = v.astype(F32)
        square = v * v
        high = square.astype(BF16)
        low = (square - high.astype(F32)).astype(BF16)
        mean = (dot(high, ones) + dot(low, ones)) * (1.0 / C)
        normed = (v * lax.rsqrt(mean + 1e-05) * gain).astype(BF16)
        joined[pl.ds(p0, step)] = dot(normed, w_qkv[...]).astype(BF16).reshape(step, B, pack * 384)
        return carry

    lax.fori_loop(0, px // step, conv_chunk, 0)

    D = pack * B
    hd = C // heads
    lane = lax.broadcasted_iota(jnp.int32, (D, 128), 1)
    srow = lax.broadcasted_iota(jnp.int32, (128, D), 0)
    factor = math.log2(math.e) / math.sqrt(hd)

    def one_pixel(p):
        t = joined[p]
        q, k, v = (
            jnp.concatenate(
                [t[:, i * 384 + g * 128 : i * 384 + (g + 1) * 128] for i in range(pack)], axis=0
            )
            for g in range(3)
        )
        keys = jnp.concatenate(
            [jnp.where(lane // hd == h, k, jnp.zeros_like(k)) for h in range(heads)], axis=0
        )
        scores = lax.dot_general(keys, q, (((1,), (1,)), ((), ())), preferred_element_type=F32)
        weights = []
        for h in range(heads):
            part = scores[h * D : (h + 1) * D]
            top = jnp.max(part, axis=0, keepdims=True)
            weights.append(jnp.exp2((part - top) * (scale_ref[h] * factor)).astype(BF16))
        weights = jnp.concatenate(weights, axis=0)
        vt = v.astype(F32).T
        values = jnp.concatenate(
            [
                jnp.where(
                    srow // hd == h, vt, jnp.where((srow - C) // hd == h, 1.0, 0.0)
                ).astype(BF16)
                for h in range(heads)
            ],
            axis=1,
        )
        o = dot(values, weights)
        o = o[:C] / o[C : 2 * C]
        if C < 128:
            o = jnp.concatenate([o, jnp.zeros((128 - C, D), F32)], axis=0)
        o = o.T.astype(BF16)
        for i in range(pack):
            mixed[p, :, i * 128 : (i + 1) * 128] = o[i * B : (i + 1) * B]

    group_px = 4 if px % 4 == 0 else 1

    def pixels(c, carry):
        for i in range(group_px):
            one_pixel(c * group_px + i)
        return carry

    lax.fori_loop(0, px // group_px, pixels, 0)

    def exit_chunk(c, carry):
        p0 = c * step
        v = second[pl.ds(p0, step)].astype(F32).reshape(step * B, LANES)
        v = v + dot(mixed[pl.ds(p0, step)].reshape(step * B, pack * 128), w_exit[...])
        v = v.astype(BF16).reshape(step, B, LANES)
        for s in range(nd):
            back[s, pl.ds(p0, step)] = v[:, s * bl : (s + 1) * bl]
        return carry

    lax.fori_loop(0, px // step, exit_chunk, 0)

    def back_copy(o):
        to = lax.rem(disp + o, nd)
        return pltpu.make_async_remote_copy(
            src_ref=back.at[to],
            dst_ref=returned.at[disp],
            send_sem=back_send.at[o - 1],
            recv_sem=back_recv.at[o - 1],
            device_id={"disp": to},
            device_id_type=MESH,
        )

    for o in range(1, nd):
        back_copy(o).start()
    returned[disp] = back[disp]
    for o in range(1, nd):
        back_copy(o).wait_recv()

    for h in range(H):
        v = returned[h // hr, (h % hr) * W : (h % hr + 1) * W].reshape(W * bl, LANES)
        v = sigmoid(dot(v, w_gate[...]) + bias_g)
        v = v * fields[0, 1 + h, 1 : W + 1].astype(F32).reshape(W * bl, LANES)
        for s in range(2):
            stage[s, h * W * bl : (h + 1) * W * bl, :] = v[:, s * 128 : (s + 1) * 128]
    for h in range(H):
        for b in range(bl):
            for s in range(2):
                out_ref[h, :, b * LANES + s * 128 : b * LANES + (s + 1) * 128] = stage[
                    s, pl.ds(h * W * bl + b, W, stride=bl), :
                ].astype(BF16)

    for k in range(layers):
        for i in range(8):
            @pl.when(exists(*DIRECTIONS[i]))
            def _():
                halo_copy(k, i).wait_send()
    for o in range(1, nd):
        there_copy(o).wait_send()
        back_copy(o).wait_send()


def per_device(axes, x, ptaps, pbias, staps, sbias, gain, qkv, wexit, scale, gate, gbias):
    nr, nd, nc = axes
    H, W, flat = x.shape
    C = ptaps.shape[-1]
    layers, taps, heads = ptaps.shape[0], staps.shape[1], scale.shape[0]
    pack = LANES // C
    bl = flat // LANES
    B = nd * bl
    px = H * W // nd
    reach = (taps // 2 + pack - 1) // pack
    sizes = (nr, nd, nc, H, W, bl, C, layers, taps, heads)
    vmem = pl.BlockSpec(memory_space=pltpu.VMEM)
    specs = [vmem] * 11
    specs[8] = pl.BlockSpec(memory_space=pltpu.SMEM)
    peers = max(nd - 1, 1)
    return pl.pallas_call(
        functools.partial(kernel, sizes),
        out_shape=jax.ShapeDtypeStruct(x.shape, x.dtype),
        in_specs=specs,
        out_specs=vmem,
        scratch_shapes=[
            pltpu.VMEM((layers, H + 2, W + 2, bl, LANES), BF16),
            pltpu.VMEM((nd, px, bl, LANES), BF16),
            pltpu.VMEM((nd, px, bl, LANES), BF16),
            pltpu.VMEM((px, B + 16, LANES), F32),
            pltpu.VMEM((px, B, LANES), BF16),
            pltpu.VMEM((px, B, pack * 384), BF16),
            pltpu.VMEM((px, B, pack * 128), BF16),
            pltpu.VMEM((nd, px, bl, LANES), BF16),
            pltpu.VMEM((nd, px, bl, LANES), BF16),
            pltpu.VMEM((2, H * W * bl, 128), F32),
            pltpu.VMEM((layers, 9 * LANES, LANES), BF16),
            pltpu.VMEM((2, (2 * reach + 1) * LANES, LANES), BF16),
            pltpu.VMEM((LANES, pack * 384), BF16),
            pltpu.VMEM((pack * 128, LANES), BF16),
            pltpu.VMEM((LANES, LANES), BF16),
            pltpu.SemaphoreType.DMA((layers, 8)),
            pltpu.SemaphoreType.DMA((layers, 8)),
            pltpu.SemaphoreType.DMA((peers,)),
            pltpu.SemaphoreType.DMA((peers,)),
            pltpu.SemaphoreType.DMA((peers,)),
            pltpu.SemaphoreType.DMA((peers,)),
        ],
        compiler_params=pltpu.CompilerParams(
            collective_id=0, has_side_effects=True, vmem_limit_bytes=48 * 1024 * 1024
        ),
    )(
        x,
        ptaps.reshape(-1, C),
        pbias,
        staps.reshape(-1, C),
        sbias,
        gain.reshape(1, C),
        qkv,
        wexit,
        scale,
        gate,
        gbias.reshape(1, C),
    )


def solution(mesh):
    axes = tuple(mesh.shape[a] for a in ("rows", "disp", "cols"))
    spec = P(("groups", "rows"), "cols", "disp")
    return jax.shard_map(
        functools.partial(per_device, axes),
        mesh=mesh,
        in_specs=(spec,) + (P(),) * 10,
        out_specs=spec,
        check_vma=False,
    )
```

```python
import functools
import math

import jax
import jax.numpy as jnp
from jax import lax
from jax.experimental import pallas as pl
from jax.experimental.pallas import tpu as pltpu
from jax.sharding import PartitionSpec as P

MESH = pl.DeviceIdType.MESH
BF16 = jnp.bfloat16
F32 = jnp.float32
LANES = 256
DIRECTIONS = [(dy, dx) for dy in (-1, 0, 1) for dx in (-1, 0, 1) if (dy, dx) != (0, 0)]


def sigmoid(v):
    return 0.5 * jnp.tanh(0.5 * v) + 0.5


def dot(a, b):
    return jnp.dot(a, b, preferred_element_type=F32)


def kernel(
    sizes,
    *refs,
):
    sources, out_ref, held, refs = refs[:11], refs[11], refs[12:23], refs[23:]
    (
        x_ref,
        plane_taps,
        plane_bias,
        shift_taps,
        shift_bias,
        gain_ref,
        qkv_ref,
        exit_ref,
        scale_ref,
        gate_ref,
        gate_bias,
    ) = held
    (
        fields,
        slabs,
        lines,
        padded,
        second,
        joined,
        mixed,
        back,
        returned,
        stage,
        w_plane,
        w_shift,
        w_qkv,
        w_exit,
        w_gate,
        halo_send,
        halo_recv,
        there_send,
        there_recv,
        back_send,
        back_recv,
        load,
    ) = refs
    nr, nd, nc, H, W, bl, C, layers, taps, heads = sizes
    pack = LANES // C
    B = nd * bl
    half = taps // 2
    reach = (half + pack - 1) // pack
    hr = H // nd
    step = 8 if W % 8 == 0 else W
    parts = W // step
    seq = list(range(1, H - 1)) + sorted({0, H - 1})
    stages = [seq[a * nd : (a + 1) * nd] for a in range(hr)]
    row, disp, col = lax.axis_index("rows"), lax.axis_index("disp"), lax.axis_index("cols")

    def exists(dy, dx):
        ok = None
        for d, at, n in ((dy, row, nr), (dx, col, nc)):
            if d == -1:
                c = at > 0
            elif d == 1:
                c = at < n - 1
            else:
                continue
            ok = c if ok is None else jnp.logical_and(ok, c)
        return ok

    loads = [pltpu.make_async_copy(a, b, load.at[i]) for i, (a, b) in enumerate(zip(sources, held))]
    for c in loads:
        c.start()

    barrier = pltpu.get_barrier_semaphore()
    expected = jnp.int32(nd - 1)
    for dy, dx in DIRECTIONS:
        here = exists(dy, dx)
        expected = expected + here.astype(jnp.int32)

        @pl.when(here)
        def _():
            pl.semaphore_signal(
                barrier, inc=1, device_id={"rows": row + dy, "cols": col + dx}, device_id_type=MESH
            )

    for o in range(1, nd):
        pl.semaphore_signal(
            barrier, inc=1, device_id={"disp": lax.rem(disp + o, nd)}, device_id_type=MESH
        )

    loads[0].wait()
    for h in range(H):
        for b in range(bl):
            block = x_ref[h, :, b * LANES : (b + 1) * LANES].astype(F32)
            for s in range(2):
                stage[s, h * bl * W + b * W : h * bl * W + (b + 1) * W, :] = block[
                    :, s * 128 : (s + 1) * 128
                ]
    for h in range(H):
        for w in range(W):
            for s in range(2):
                fields[0, 1 + h, 1 + w, :, s * 128 : (s + 1) * 128] = stage[
                    s, pl.ds(h * bl * W + w, bl, stride=W), :
                ].astype(BF16)

    pl.semaphore_wait(barrier, expected)

    def span(d, n):
        return slice(1, n + 1) if d == 0 else (slice(1, 2) if d == -1 else slice(n, n + 1))

    def landing(d, n):
        return slice(1, n + 1) if d == 0 else (slice(n + 1, n + 2) if d == -1 else slice(0, 1))

    def halo_copy(k, i):
        dy, dx = DIRECTIONS[i]
        return pltpu.make_async_remote_copy(
            src_ref=fields.at[k, span(dy, H), span(dx, W)],
            dst_ref=fields.at[k, landing(dy, H), landing(dx, W)],
            send_sem=halo_send.at[k, i],
            recv_sem=halo_recv.at[k, i],
            device_id={"rows": row + dy, "cols": col + dx},
            device_id_type=MESH,
        )

    order = sorted(range(8), key=lambda i: DIRECTIONS[i][1] != 0)

    def halo_start(k, sides):
        for i in order:
            if DIRECTIONS[i][0] not in sides:
                continue

            @pl.when(exists(*DIRECTIONS[i]))
            def _():
                halo_copy(k, i).start()

    def halo_wait(k, which):
        for i in which:
            dy, dx = DIRECTIONS[i]

            @pl.when(exists(-dy, -dx))
            def _():
                halo_copy(k, i).wait_recv()

    halo_start(0, (-1, 0, 1))

    for i in range(8):
        dy, dx = DIRECTIONS[i]

        @pl.when(jnp.logical_not(exists(-dy, -dx)))
        def _():
            for k in range(layers):
                view = fields.at[k, landing(dy, H), landing(dx, W)]
                view[...] = jnp.zeros(view.shape, BF16)

    r_at = lax.broadcasted_iota(jnp.int32, (C, LANES), 0)
    l_at = lax.broadcasted_iota(jnp.int32, (C, LANES), 1)
    repeat = (l_at % C == r_at).astype(BF16)
    group = l_at // C

    def spread(w):
        return dot(w, repeat)

    for c in loads[1:]:
        c.wait()

    def plane_weights(l):
        for t in range(9):
            wide = spread(plane_taps[(l * 9 + t) * C : (l * 9 + t + 1) * C, :])
            for i in range(pack):
                at = t * LANES + i * C
                w_plane[l, at : at + C, :] = jnp.where(group == i, wide, 0.0).astype(BF16)

    bias_p = jnp.concatenate([plane_bias[...]] * pack, axis=1)
    bias_s = jnp.concatenate([shift_bias[...]] * pack, axis=1)
    bias_g = jnp.concatenate([gate_bias[...]] * pack, axis=1)
    gain = jnp.concatenate([gain_ref[...]] * pack, axis=1)

    def shift_weights(l):
        wides = [
            spread(shift_taps[(l * taps + t) * C : (l * taps + t + 1) * C, :]) for t in range(taps)
        ]
        for j in range(-reach, reach + 1):
            for i in range(pack):
                value = jnp.zeros((C, LANES), F32)
                for o in range(pack):
                    t = pack * j + i - o + half
                    if 0 <= t < taps:
                        value = jnp.where(group == o, wides[t], value)
                at = (j + reach) * LANES + i * C
                w_shift[l, at : at + C, :] = value.astype(BF16)

    def small_weights():
        a = lax.broadcasted_iota(jnp.int32, (3 * C, 3 * 128), 0)
        b = lax.broadcasted_iota(jnp.int32, (3 * C, 3 * 128), 1)
        place = jnp.logical_and(a // C == b // 128, a % C == b % 128).astype(BF16)
        wide = dot(qkv_ref[...], place).astype(BF16)
        w_qkv[...] = jnp.zeros(w_qkv.shape, BF16)
        for i in range(pack):
            w_qkv[i * C : (i + 1) * C, i * 384 : (i + 1) * 384] = wide
        w_exit[...] = jnp.zeros(w_exit.shape, BF16)
        wide = spread(exit_ref[...])
        for i in range(pack):
            w_exit[i * 128 : i * 128 + C, :] = jnp.where(group == i, wide, 0.0).astype(BF16)
        wide = spread(gate_ref[...])
        for i in range(pack):
            w_gate[i * C : (i + 1) * C, :] = jnp.where(group == i, wide, 0.0).astype(BF16)
        padded[:, 0:8, :] = jnp.zeros((W, 8, LANES), F32)
        padded[:, B + 8 : B + 16, :] = jnp.zeros((W, 8, LANES), F32)

    def there_copy(a, o):
        to = lax.rem(disp + o, nd)
        return pltpu.make_async_remote_copy(
            src_ref=slabs.at[a, to],
            dst_ref=lines.at[a, disp],
            send_sem=there_send.at[a, o - 1],
            recv_sem=there_recv.at[a, o - 1],
            device_id={"disp": to},
            device_id_type=MESH,
        )

    def plane_row(k, h, slot=None):
        lhs = jnp.concatenate(
            [
                fields[k, h + dy, dx : dx + W].reshape(W * bl, LANES)
                for dy in range(3)
                for dx in range(3)
            ],
            axis=1,
        )
        v = dot(lhs, w_plane[k]) + bias_p[k : k + 1]
        v = (v * sigmoid(v)).astype(BF16).reshape(W, bl, LANES)
        if k + 1 < layers:
            fields[k + 1, 1 + h, 1 : W + 1] = v
        else:
            slabs[slot] = v

    sides = [i for i in range(8) if DIRECTIONS[i][0] == 0]
    below = [i for i in range(8) if DIRECTIONS[i][0] == -1]
    above = [i for i in range(8) if DIRECTIONS[i][0] == 1]
    plane_weights(0)
    for k in range(layers - 1):
        halo_wait(k, sides)
        for h in range(1, H - 1):
            plane_row(k, h)
        plane_weights(k + 1)
        if k == 0:
            small_weights()
        if k == layers - 2:
            shift_weights(0)
        halo_wait(k, above)
        if H > 1:
            plane_row(k, 0)
            halo_start(k + 1, (-1,))
        halo_wait(k, below)
        plane_row(k, H - 1)
        halo_start(k + 1, (1, 0) if H > 1 else (-1, 1, 0))

    k = layers - 1
    halo_wait(k, sides)
    waited = False
    for a, rows_here in enumerate(stages):
        inner = [h for h in rows_here if 0 < h < H - 1]
        outer = [h for h in rows_here if not 0 < h < H - 1]
        if outer and not inner and not waited:
            shift_weights(1)
            halo_wait(k, above + below)
            waited = True
        if len(inner) == nd or len(outer) == nd == 2:
            for o in list(range(1, nd)) + [0]:
                q = lax.rem(disp + o, nd)
                h = 1 + a * nd + q if inner else q * (H - 1)
                plane_row(k, h, (a, q))
                if o:
                    there_copy(a, o).start()
        else:
            for h in inner:
                plane_row(k, h, (a, rows_here.index(h)))
            if outer and not waited:
                shift_weights(1)
                halo_wait(k, above + below)
                waited = True
            for h in outer:
                plane_row(k, h, (a, rows_here.index(h)))
            for o in range(1, nd):
                there_copy(a, o).start()
        lines[a, disp] = slabs[a, disp]

    def shift_conv(l, p0):
        lhs = jnp.concatenate(
            [
                padded[pl.ds(p0, step), 8 + j : 8 + j + B, :].astype(BF16).reshape(step * B, LANES)
                for j in range(-reach, reach + 1)
            ],
            axis=1,
        )
        return dot(lhs, w_shift[l]) + bias_s[l : l + 1]

    ones_a = lax.broadcasted_iota(jnp.int32, (LANES, LANES), 0) // C
    ones_b = lax.broadcasted_iota(jnp.int32, (LANES, LANES), 1) // C
    ones = (ones_a == ones_b).astype(BF16)

    def conv_chunk(p0):
        v = shift_conv(0, p0)
        v = (v * sigmoid(v)).astype(BF16).astype(F32)
        padded[pl.ds(p0, step), 8 : 8 + B, :] = v.reshape(step, B, LANES)
        v = shift_conv(1, p0).astype(BF16)
        second[pl.ds(p0, step)] = v.reshape(step, B, LANES)
        v = v.astype(F32)
        square = v * v
        high = square.astype(BF16)
        low = (square - high.astype(F32)).astype(BF16)
        mean = (dot(high, ones) + dot(low, ones)) * (1.0 / C)
        normed = (v * lax.rsqrt(mean + 1e-05) * gain).astype(BF16)
        joined[pl.ds(p0, step)] = dot(normed, w_qkv[...]).astype(BF16).reshape(step, B, pack * 384)

    D = pack * B
    hd = C // heads
    lane = lax.broadcasted_iota(jnp.int32, (D, 128), 1)
    together = LANES // D if heads % max(LANES // D, 1) == 0 else 1
    together = max(together, 1)
    factor = math.log2(math.e) / math.sqrt(hd)
    ones_rows = jnp.ones((16, D), BF16)
    scales = [
        jnp.concatenate(
            [
                jnp.broadcast_to(scale_ref[:, h : h + 1] * factor, (1, D))
                for h in range(g, g + together)
            ],
            axis=1,
        )
        for g in range(0, heads, together)
    ]

    def one_pixel(p):
        t = joined[p]
        q, k, v = (
            jnp.concatenate(
                [t[:, i * 384 + g * 128 : i * 384 + (g + 1) * 128] for i in range(pack)], axis=0
            )
            for g in range(3)
        )
        vt = v.astype(F32).T.astype(BF16)
        outs = []
        for n, g in enumerate(range(0, heads, together)):
            queries = jnp.concatenate(
                [
                    jnp.where(lane // hd == h, q, jnp.zeros_like(q))
                    for h in range(g, g + together)
                ],
                axis=0,
            )
            scores = lax.dot_general(
                k, queries, (((1,), (1,)), ((), ())), preferred_element_type=F32
            )
            top = jnp.max(scores, axis=0, keepdims=True)
            weights = jnp.exp2((scores - top) * scales[n]).astype(BF16)
            values = jnp.concatenate([vt[g * hd : (g + together) * hd], ones_rows], axis=0)
            o = dot(values, weights)
            inverse = 1.0 / o[together * hd : together * hd + 1]
            for i in range(together):
                cut = slice(i * D, (i + 1) * D)
                outs.append(o[i * hd : (i + 1) * hd, cut] * inverse[:, cut])
        o = jnp.concatenate(outs, axis=0)
        if C < 128:
            o = jnp.concatenate([o, jnp.zeros((128 - C, D), F32)], axis=0)
        o = o.T.astype(BF16)
        for i in range(pack):
            mixed[p, :, i * 128 : (i + 1) * 128] = o[i * B : (i + 1) * B]

    group_px = 4 if step % 4 == 0 else 1

    def back_copy(a, part, o):
        to = lax.rem(disp + o, nd)
        cut = pl.ds(part * step, step)
        return pltpu.make_async_remote_copy(
            src_ref=back.at[a, to, cut],
            dst_ref=returned.at[a, disp, cut],
            send_sem=back_send.at[a, part, o - 1],
            recv_sem=back_recv.at[a, part, o - 1],
            device_id={"disp": to},
            device_id_type=MESH,
        )

    def exit_chunk(a, p0):
        v = second[pl.ds(p0, step)].astype(F32).reshape(step * B, LANES)
        v = v + dot(mixed[pl.ds(p0, step)].reshape(step * B, pack * 128), w_exit[...])
        v = v.astype(BF16).reshape(step, B, LANES)
        for s in range(nd):
            back[a, s, pl.ds(p0, step)] = v[:, s * bl : (s + 1) * bl]
        returned[a, disp, pl.ds(p0, step)] = back[a, disp, pl.ds(p0, step)]

    for a in range(hr):
        for o in range(1, nd):
            there_copy(a, o).wait_recv()
        for s in range(nd):
            padded[:, 8 + s * bl : 8 + (s + 1) * bl, :] = lines[a, s].astype(F32)

        def one_part(part, carry):
            p0 = part * step
            conv_chunk(p0)

            def pixels(c, inner):
                for i in range(group_px):
                    one_pixel(p0 + c * group_px + i)
                return inner

            lax.fori_loop(0, step // group_px, pixels, 0)
            exit_chunk(a, p0)
            for o in range(1, nd):
                back_copy(a, part, o).start()
            return carry

        lax.fori_loop(0, parts, one_part, 0)

    for a, rows_here in enumerate(stages):
        for part in range(parts):
            for o in range(1, nd):
                back_copy(a, part, o).wait_recv()
            for n, h in enumerate(rows_here):
                w0 = part * step
                v = returned[a, n, w0 : w0 + step].reshape(step * bl, LANES)
                v = sigmoid(dot(v, w_gate[...]) + bias_g)
                x = fields[0, 1 + h, 1 + w0 : 1 + w0 + step].astype(F32)
                v = v * x.reshape(step * bl, LANES)
                at = (h * W + w0) * bl
                for s in range(2):
                    stage[s, at : at + step * bl, :] = v[:, s * 128 : (s + 1) * 128]
        for h in rows_here:
            for b in range(bl):
                for s in range(2):
                    out_ref[h, :, b * LANES + s * 128 : b * LANES + (s + 1) * 128] = stage[
                        s, pl.ds(h * W * bl + b, W, stride=bl), :
                    ].astype(BF16)

    for k in range(layers):
        for i in range(8):
            @pl.when(exists(*DIRECTIONS[i]))
            def _():
                halo_copy(k, i).wait_send()
    for o in range(1, nd):
        for a in range(hr):
            there_copy(a, o).wait_send()
            for part in range(parts):
                back_copy(a, part, o).wait_send()


def per_device(axes, x, ptaps, pbias, staps, sbias, gain, qkv, wexit, scale, gate, gbias):
    nr, nd, nc = axes
    H, W, flat = x.shape
    C = ptaps.shape[-1]
    layers, taps, heads = ptaps.shape[0], staps.shape[1], scale.shape[0]
    pack = LANES // C
    bl = flat // LANES
    B = nd * bl
    hr = H // nd
    parts = W // 8 if W % 8 == 0 else 1
    reach = (taps // 2 + pack - 1) // pack
    sizes = (nr, nd, nc, H, W, bl, C, layers, taps, heads)
    peers = max(nd - 1, 1)
    arguments = (
        x,
        ptaps.reshape(-1, C),
        pbias,
        staps.reshape(-1, C),
        sbias,
        gain.reshape(1, C),
        qkv,
        wexit,
        scale.reshape(1, heads),
        gate,
        gbias.reshape(1, C),
    )
    return pl.pallas_call(
        functools.partial(kernel, sizes),
        out_shape=jax.ShapeDtypeStruct(x.shape, x.dtype),
        in_specs=[pl.BlockSpec(memory_space=pltpu.HBM)] * len(arguments),
        out_specs=pl.BlockSpec(memory_space=pltpu.VMEM),
        scratch_shapes=[pltpu.VMEM(v.shape, v.dtype) for v in arguments]
        + [
            pltpu.VMEM((layers, H + 2, W + 2, bl, LANES), BF16),
            pltpu.VMEM((hr, nd, W, bl, LANES), BF16),
            pltpu.VMEM((hr, nd, W, bl, LANES), BF16),
            pltpu.VMEM((W, B + 16, LANES), F32),
            pltpu.VMEM((W, B, LANES), BF16),
            pltpu.VMEM((W, B, pack * 384), BF16),
            pltpu.VMEM((W, B, pack * 128), BF16),
            pltpu.VMEM((hr, nd, W, bl, LANES), BF16),
            pltpu.VMEM((hr, nd, W, bl, LANES), BF16),
            pltpu.VMEM((2, H * W * bl, 128), F32),
            pltpu.VMEM((layers, 9 * LANES, LANES), BF16),
            pltpu.VMEM((2, (2 * reach + 1) * LANES, LANES), BF16),
            pltpu.VMEM((LANES, pack * 384), BF16),
            pltpu.VMEM((pack * 128, LANES), BF16),
            pltpu.VMEM((LANES, LANES), BF16),
            pltpu.SemaphoreType.DMA((layers, 8)),
            pltpu.SemaphoreType.DMA((layers, 8)),
            pltpu.SemaphoreType.DMA((hr, peers)),
            pltpu.SemaphoreType.DMA((hr, peers)),
            pltpu.SemaphoreType.DMA((hr, parts, peers)),
            pltpu.SemaphoreType.DMA((hr, parts, peers)),
            pltpu.SemaphoreType.DMA((len(arguments),)),
        ],
        compiler_params=pltpu.CompilerParams(
            collective_id=0, has_side_effects=True, vmem_limit_bytes=48 * 1024 * 1024
        ),
    )(*arguments)


def solution(mesh):
    axes = tuple(mesh.shape[a] for a in ("rows", "disp", "cols"))
    spec = P(("groups", "rows"), "cols", "disp")
    return jax.shard_map(
        functools.partial(per_device, axes),
        mesh=mesh,
        in_specs=(spec,) + (P(),) * 10,
        out_specs=spec,
        check_vma=False,
    )
```

```python
import functools
import math

import jax
import jax.numpy as jnp
from jax import lax
from jax.experimental import pallas as pl
from jax.experimental.pallas import tpu as pltpu
from jax.sharding import PartitionSpec as P

MESH = pl.DeviceIdType.MESH
BF16 = jnp.bfloat16
F32 = jnp.float32
LANES = 256
DIRECTIONS = [(dy, dx) for dy in (-1, 0, 1) for dx in (-1, 0, 1) if (dy, dx) != (0, 0)]


def sigmoid(v):
    return 0.5 * jnp.tanh(0.5 * v) + 0.5


def dot(a, b):
    return jnp.dot(a, b, preferred_element_type=F32)


def kernel(
    sizes,
    *refs,
):
    sources, out_ref, held, refs = refs[:11], refs[11], refs[12:23], refs[23:]
    (
        x_ref,
        plane_taps,
        plane_bias,
        shift_taps,
        shift_bias,
        gain_ref,
        qkv_ref,
        exit_ref,
        scale_ref,
        gate_ref,
        gate_bias,
    ) = held
    (
        fields,
        slabs,
        lines,
        padded,
        second,
        joined,
        mixed,
        back,
        returned,
        stage,
        w_plane,
        w_shift,
        w_qkv,
        w_exit,
        w_gate,
        halo_send,
        halo_recv,
        there_send,
        there_recv,
        back_send,
        back_recv,
        load,
    ) = refs
    nr, nd, nc, H, W, bl, C, layers, taps, heads = sizes
    pack = LANES // C
    B = nd * bl
    half = taps // 2
    reach = (half + pack - 1) // pack
    hr = H // nd
    step = 8 if W % 8 == 0 else W
    parts = W // step
    seq = list(range(1, H - 1)) + sorted({0, H - 1})
    stages = [seq[a * nd : (a + 1) * nd] for a in range(hr)]
    row, disp, col = lax.axis_index("rows"), lax.axis_index("disp"), lax.axis_index("cols")

    def exists(dy, dx):
        ok = None
        for d, at, n in ((dy, row, nr), (dx, col, nc)):
            if d == -1:
                c = at > 0
            elif d == 1:
                c = at < n - 1
            else:
                continue
            ok = c if ok is None else jnp.logical_and(ok, c)
        return ok

    loads = [pltpu.make_async_copy(a, b, load.at[i]) for i, (a, b) in enumerate(zip(sources, held))]
    for c in loads:
        c.start()

    barrier = pltpu.get_barrier_semaphore()
    expected = jnp.int32(nd - 1)
    for dy, dx in DIRECTIONS:
        here = exists(dy, dx)
        expected = expected + here.astype(jnp.int32)

        @pl.when(here)
        def _():
            pl.semaphore_signal(
                barrier, inc=1, device_id={"rows": row + dy, "cols": col + dx}, device_id_type=MESH
            )

    for o in range(1, nd):
        pl.semaphore_signal(
            barrier, inc=1, device_id={"disp": lax.rem(disp + o, nd)}, device_id_type=MESH
        )

    loads[0].wait()
    for h in range(H):
        for b in range(bl):
            block = x_ref[h, :, b * LANES : (b + 1) * LANES].astype(F32)
            for s in range(2):
                stage[s, h * bl * W + b * W : h * bl * W + (b + 1) * W, :] = block[
                    :, s * 128 : (s + 1) * 128
                ]
    for h in range(H):
        for w in range(W):
            for s in range(2):
                fields[0, 1 + h, 1 + w, :, s * 128 : (s + 1) * 128] = stage[
                    s, pl.ds(h * bl * W + w, bl, stride=W), :
                ].astype(BF16)

    pl.semaphore_wait(barrier, expected)

    def span(d, n):
        return slice(1, n + 1) if d == 0 else (slice(1, 2) if d == -1 else slice(n, n + 1))

    def landing(d, n):
        return slice(1, n + 1) if d == 0 else (slice(n + 1, n + 2) if d == -1 else slice(0, 1))

    def halo_copy(k, i):
        dy, dx = DIRECTIONS[i]
        return pltpu.make_async_remote_copy(
            src_ref=fields.at[k, span(dy, H), span(dx, W)],
            dst_ref=fields.at[k, landing(dy, H), landing(dx, W)],
            send_sem=halo_send.at[k, i],
            recv_sem=halo_recv.at[k, i],
            device_id={"rows": row + dy, "cols": col + dx},
            device_id_type=MESH,
        )

    order = sorted(range(8), key=lambda i: DIRECTIONS[i][1] != 0)

    def halo_start(k, sides):
        for i in order:
            if DIRECTIONS[i][0] not in sides:
                continue

            @pl.when(exists(*DIRECTIONS[i]))
            def _():
                halo_copy(k, i).start()

    def halo_wait(k, which):
        for i in which:
            dy, dx = DIRECTIONS[i]

            @pl.when(exists(-dy, -dx))
            def _():
                halo_copy(k, i).wait_recv()

    halo_start(0, (-1, 0, 1))

    for i in range(8):
        dy, dx = DIRECTIONS[i]

        @pl.when(jnp.logical_not(exists(-dy, -dx)))
        def _():
            for k in range(layers):
                view = fields.at[k, landing(dy, H), landing(dx, W)]
                view[...] = jnp.zeros(view.shape, BF16)

    r_at = lax.broadcasted_iota(jnp.int32, (C, LANES), 0)
    l_at = lax.broadcasted_iota(jnp.int32, (C, LANES), 1)
    repeat = (l_at % C == r_at).astype(BF16)
    group = l_at // C

    def spread(w):
        return dot(w, repeat)

    for c in loads[1:]:
        c.wait()

    def plane_weights(l):
        for t in range(9):
            wide = spread(plane_taps[(l * 9 + t) * C : (l * 9 + t + 1) * C, :])
            for i in range(pack):
                at = t * LANES + i * C
                w_plane[l, at : at + C, :] = jnp.where(group == i, wide, 0.0).astype(BF16)

    bias_p = jnp.concatenate([plane_bias[...]] * pack, axis=1)
    bias_s = jnp.concatenate([shift_bias[...]] * pack, axis=1)
    bias_g = jnp.concatenate([gate_bias[...]] * pack, axis=1)
    gain = jnp.concatenate([gain_ref[...]] * pack, axis=1)

    def shift_weights(l):
        wides = [
            spread(shift_taps[(l * taps + t) * C : (l * taps + t + 1) * C, :]) for t in range(taps)
        ]
        for j in range(-reach, reach + 1):
            for i in range(pack):
                value = jnp.zeros((C, LANES), F32)
                for o in range(pack):
                    t = pack * j + i - o + half
                    if 0 <= t < taps:
                        value = jnp.where(group == o, wides[t], value)
                at = (j + reach) * LANES + i * C
                w_shift[l, at : at + C, :] = value.astype(BF16)

    def small_weights():
        a = lax.broadcasted_iota(jnp.int32, (3 * C, 3 * 128), 0)
        b = lax.broadcasted_iota(jnp.int32, (3 * C, 3 * 128), 1)
        place = jnp.logical_and(a // C == b // 128, a % C == b % 128).astype(BF16)
        wide = dot(qkv_ref[...], place).astype(BF16)
        w_qkv[...] = jnp.zeros(w_qkv.shape, BF16)
        for i in range(pack):
            w_qkv[i * C : (i + 1) * C, i * 384 : (i + 1) * 384] = wide
        w_exit[...] = jnp.zeros(w_exit.shape, BF16)
        wide = spread(exit_ref[...])
        for i in range(pack):
            w_exit[i * 128 : i * 128 + C, :] = jnp.where(group == i, wide, 0.0).astype(BF16)
        wide = spread(gate_ref[...])
        for i in range(pack):
            w_gate[i * C : (i + 1) * C, :] = jnp.where(group == i, wide, 0.0).astype(BF16)
        padded[:, 0:8, :] = jnp.zeros((W, 8, LANES), F32)
        padded[:, B + 8 : B + 16, :] = jnp.zeros((W, 8, LANES), F32)

    def there_copy(a, o):
        to = lax.rem(disp + o, nd)
        return pltpu.make_async_remote_copy(
            src_ref=slabs.at[a, to],
            dst_ref=lines.at[a, disp],
            send_sem=there_send.at[a, o - 1],
            recv_sem=there_recv.at[a, o - 1],
            device_id={"disp": to},
            device_id_type=MESH,
        )

    def plane_rows(k, h, n):
        lhs = jnp.concatenate(
            [
                fields[k, pl.ds(h + dy, n), dx : dx + W].reshape(n * W * bl, LANES)
                for dy in range(3)
                for dx in range(3)
            ],
            axis=1,
        )
        v = dot(lhs, w_plane[k]) + bias_p[k : k + 1]
        return (v * sigmoid(v)).astype(BF16).reshape(n, W, bl, LANES)

    def plane_row(k, h, slot=None, n=1):
        v = plane_rows(k, h, n)
        if k + 1 < layers:
            fields[k + 1, 1 + h : 1 + h + n, 1 : W + 1] = v
        else:
            slabs[slot] = v[0]

    sides = [i for i in range(8) if DIRECTIONS[i][0] == 0]
    below = [i for i in range(8) if DIRECTIONS[i][0] == -1]
    above = [i for i in range(8) if DIRECTIONS[i][0] == 1]
    plane_weights(0)
    for k in range(layers - 1):
        halo_wait(k, sides)
        if H > 2:
            plane_row(k, 1, n=H - 2)
        plane_weights(k + 1)
        if k == 0:
            small_weights()
        if k == layers - 2:
            shift_weights(0)
        halo_wait(k, above)
        if H > 1:
            plane_row(k, 0)
            halo_start(k + 1, (-1,))
        halo_wait(k, below)
        plane_row(k, H - 1)
        halo_start(k + 1, (1, 0) if H > 1 else (-1, 1, 0))

    k = layers - 1
    halo_wait(k, sides)
    waited = False
    for a, rows_here in enumerate(stages):
        inner = [h for h in rows_here if 0 < h < H - 1]
        outer = [h for h in rows_here if not 0 < h < H - 1]
        if outer and not inner and not waited:
            shift_weights(1)
            halo_wait(k, above + below)
            waited = True
        if len(inner) == nd == H - 2:
            v = plane_rows(k, 1, nd)
            for n in range(nd):
                slabs[a, n] = v[n]
            for o in range(1, nd):
                there_copy(a, o).start()
        elif len(inner) == nd or len(outer) == nd == 2:
            for o in list(range(1, nd)) + [0]:
                q = lax.rem(disp + o, nd)
                h = 1 + a * nd + q if inner else q * (H - 1)
                plane_row(k, h, (a, q))
                if o:
                    there_copy(a, o).start()
        else:
            for h in inner:
                plane_row(k, h, (a, rows_here.index(h)))
            if outer and not waited:
                shift_weights(1)
                halo_wait(k, above + below)
                waited = True
            for h in outer:
                plane_row(k, h, (a, rows_here.index(h)))
            for o in range(1, nd):
                there_copy(a, o).start()
        lines[a, disp] = slabs[a, disp]

    def shift_conv(l):
        lhs = jnp.concatenate(
            [
                padded[:, 8 + j : 8 + j + B, :].astype(BF16).reshape(W * B, LANES)
                for j in range(-reach, reach + 1)
            ],
            axis=1,
        )
        return dot(lhs, w_shift[l]) + bias_s[l : l + 1]

    ones_a = lax.broadcasted_iota(jnp.int32, (LANES, LANES), 0) // C
    ones_b = lax.broadcasted_iota(jnp.int32, (LANES, LANES), 1) // C
    ones = (ones_a == ones_b).astype(BF16)

    def conv_rows():
        v = shift_conv(0)
        v = (v * sigmoid(v)).astype(BF16).astype(F32)
        padded[:, 8 : 8 + B, :] = v.reshape(W, B, LANES)
        v = shift_conv(1).astype(BF16)
        second[...] = v.reshape(W, B, LANES)
        v = v.astype(F32)
        square = v * v
        high = square.astype(BF16)
        low = (square - high.astype(F32)).astype(BF16)
        mean = (dot(high, ones) + dot(low, ones)) * (1.0 / C)
        normed = (v * lax.rsqrt(mean + 1e-05) * gain).astype(BF16)
        joined[...] = dot(normed, w_qkv[...]).astype(BF16).reshape(W, B, pack * 384)

    D = pack * B
    hd = C // heads
    lane = lax.broadcasted_iota(jnp.int32, (D, 128), 1)
    together = LANES // D if heads % max(LANES // D, 1) == 0 else 1
    together = max(together, 1)
    factor = math.log2(math.e) / math.sqrt(hd)
    ones_rows = jnp.ones((16, D), BF16)
    scales = [
        jnp.concatenate(
            [
                jnp.broadcast_to(scale_ref[:, h : h + 1] * factor, (1, D))
                for h in range(g, g + together)
            ],
            axis=1,
        )
        for g in range(0, heads, together)
    ]

    def one_pixel(p):
        t = joined[p]
        q, k, v = (
            jnp.concatenate(
                [t[:, i * 384 + g * 128 : i * 384 + (g + 1) * 128] for i in range(pack)], axis=0
            )
            for g in range(3)
        )
        vt = v.astype(F32).T.astype(BF16)
        outs = []
        for n, g in enumerate(range(0, heads, together)):
            queries = jnp.concatenate(
                [
                    jnp.where(lane // hd == h, q, jnp.zeros_like(q))
                    for h in range(g, g + together)
                ],
                axis=0,
            )
            scores = lax.dot_general(
                k, queries, (((1,), (1,)), ((), ())), preferred_element_type=F32
            )
            top = jnp.max(scores, axis=0, keepdims=True)
            weights = jnp.exp2((scores - top) * scales[n]).astype(BF16)
            values = jnp.concatenate([vt[g * hd : (g + together) * hd], ones_rows], axis=0)
            o = dot(values, weights)
            inverse = 1.0 / o[together * hd : together * hd + 1]
            for i in range(together):
                cut = slice(i * D, (i + 1) * D)
                outs.append(o[i * hd : (i + 1) * hd, cut] * inverse[:, cut])
        o = jnp.concatenate(outs, axis=0)
        if C < 128:
            o = jnp.concatenate([o, jnp.zeros((128 - C, D), F32)], axis=0)
        o = o.T.astype(BF16)
        for i in range(pack):
            mixed[p, :, i * 128 : (i + 1) * 128] = o[i * B : (i + 1) * B]

    group_px = 8 if step % 8 == 0 else 1

    def back_copy(a, part, o):
        to = lax.rem(disp + o, nd)
        cut = pl.ds(part * step, step)
        return pltpu.make_async_remote_copy(
            src_ref=back.at[a, to, cut],
            dst_ref=returned.at[a, disp, cut],
            send_sem=back_send.at[a, part, o - 1],
            recv_sem=back_recv.at[a, part, o - 1],
            device_id={"disp": to},
            device_id_type=MESH,
        )

    def exit_chunk(a, p0):
        v = second[pl.ds(p0, step)].astype(F32).reshape(step * B, LANES)
        v = v + dot(mixed[pl.ds(p0, step)].reshape(step * B, pack * 128), w_exit[...])
        v = v.astype(BF16).reshape(step, B, LANES)
        for s in range(nd):
            back[a, s, pl.ds(p0, step)] = v[:, s * bl : (s + 1) * bl]
        returned[a, disp, pl.ds(p0, step)] = back[a, disp, pl.ds(p0, step)]

    for a in range(hr):
        for o in range(1, nd):
            there_copy(a, o).wait_recv()
        for s in range(nd):
            padded[:, 8 + s * bl : 8 + (s + 1) * bl, :] = lines[a, s].astype(F32)

        conv_rows()

        def one_part(part, carry):
            p0 = part * step

            def pixels(c, inner):
                for i in range(group_px):
                    one_pixel(p0 + c * group_px + i)
                return inner

            lax.fori_loop(0, step // group_px, pixels, 0)
            exit_chunk(a, p0)
            for o in range(1, nd):
                back_copy(a, part, o).start()
            return carry

        lax.fori_loop(0, parts, one_part, 0)

    for a, rows_here in enumerate(stages):
        for part in range(parts):
            for o in range(1, nd):
                back_copy(a, part, o).wait_recv()
            for n, h in enumerate(rows_here):
                w0 = part * step
                v = returned[a, n, w0 : w0 + step].reshape(step * bl, LANES)
                v = sigmoid(dot(v, w_gate[...]) + bias_g)
                x = fields[0, 1 + h, 1 + w0 : 1 + w0 + step].astype(F32)
                v = v * x.reshape(step * bl, LANES)
                at = (h * W + w0) * bl
                for s in range(2):
                    stage[s, at : at + step * bl, :] = v[:, s * 128 : (s + 1) * 128]
        for h in rows_here:
            for b in range(bl):
                for s in range(2):
                    out_ref[h, :, b * LANES + s * 128 : b * LANES + (s + 1) * 128] = stage[
                        s, pl.ds(h * W * bl + b, W, stride=bl), :
                    ].astype(BF16)

    for k in range(layers):
        for i in range(8):
            @pl.when(exists(*DIRECTIONS[i]))
            def _():
                halo_copy(k, i).wait_send()
    for o in range(1, nd):
        for a in range(hr):
            there_copy(a, o).wait_send()
            for part in range(parts):
                back_copy(a, part, o).wait_send()


def per_device(axes, x, ptaps, pbias, staps, sbias, gain, qkv, wexit, scale, gate, gbias):
    nr, nd, nc = axes
    H, W, flat = x.shape
    C = ptaps.shape[-1]
    layers, taps, heads = ptaps.shape[0], staps.shape[1], scale.shape[0]
    pack = LANES // C
    bl = flat // LANES
    B = nd * bl
    hr = H // nd
    parts = W // 8 if W % 8 == 0 else 1
    reach = (taps // 2 + pack - 1) // pack
    sizes = (nr, nd, nc, H, W, bl, C, layers, taps, heads)
    peers = max(nd - 1, 1)
    arguments = (
        x,
        ptaps.reshape(-1, C),
        pbias,
        staps.reshape(-1, C),
        sbias,
        gain.reshape(1, C),
        qkv,
        wexit,
        scale.reshape(1, heads),
        gate,
        gbias.reshape(1, C),
    )
    return pl.pallas_call(
        functools.partial(kernel, sizes),
        out_shape=jax.ShapeDtypeStruct(x.shape, x.dtype),
        in_specs=[pl.BlockSpec(memory_space=pltpu.HBM)] * len(arguments),
        out_specs=pl.BlockSpec(memory_space=pltpu.VMEM),
        scratch_shapes=[pltpu.VMEM(v.shape, v.dtype) for v in arguments]
        + [
            pltpu.VMEM((layers, H + 2, W + 2, bl, LANES), BF16),
            pltpu.VMEM((hr, nd, W, bl, LANES), BF16),
            pltpu.VMEM((hr, nd, W, bl, LANES), BF16),
            pltpu.VMEM((W, B + 16, LANES), F32),
            pltpu.VMEM((W, B, LANES), BF16),
            pltpu.VMEM((W, B, pack * 384), BF16),
            pltpu.VMEM((W, B, pack * 128), BF16),
            pltpu.VMEM((hr, nd, W, bl, LANES), BF16),
            pltpu.VMEM((hr, nd, W, bl, LANES), BF16),
            pltpu.VMEM((2, H * W * bl, 128), F32),
            pltpu.VMEM((layers, 9 * LANES, LANES), BF16),
            pltpu.VMEM((2, (2 * reach + 1) * LANES, LANES), BF16),
            pltpu.VMEM((LANES, pack * 384), BF16),
            pltpu.VMEM((pack * 128, LANES), BF16),
            pltpu.VMEM((LANES, LANES), BF16),
            pltpu.SemaphoreType.DMA((layers, 8)),
            pltpu.SemaphoreType.DMA((layers, 8)),
            pltpu.SemaphoreType.DMA((hr, peers)),
            pltpu.SemaphoreType.DMA((hr, peers)),
            pltpu.SemaphoreType.DMA((hr, parts, peers)),
            pltpu.SemaphoreType.DMA((hr, parts, peers)),
            pltpu.SemaphoreType.DMA((len(arguments),)),
        ],
        compiler_params=pltpu.CompilerParams(
            collective_id=0, has_side_effects=True, vmem_limit_bytes=63 * 1024 * 1024
        ),
    )(*arguments)


def solution(mesh):
    axes = tuple(mesh.shape[a] for a in ("rows", "disp", "cols"))
    spec = P(("groups", "rows"), "cols", "disp")
    return jax.shard_map(
        functools.partial(per_device, axes),
        mesh=mesh,
        in_specs=(spec,) + (P(),) * 10,
        out_specs=spec,
        check_vma=False,
    )
```

```python
import functools
import math

import jax
import jax.numpy as jnp
from jax import lax
from jax.experimental import pallas as pl
from jax.experimental.pallas import tpu as pltpu
from jax.sharding import PartitionSpec as P

MESH = pl.DeviceIdType.MESH
BF16 = jnp.bfloat16
F32 = jnp.float32
LANES = 256
DIRECTIONS = [(dy, dx) for dy in (-1, 0, 1) for dx in (-1, 0, 1) if (dy, dx) != (0, 0)]


def sigmoid(v):
    return 0.5 * jnp.tanh(0.5 * v) + 0.5


def dot(a, b):
    return jnp.dot(a, b, preferred_element_type=F32)


def kernel(
    sizes,
    *refs,
):
    sources, out_ref, held, refs = refs[:11], refs[11], refs[12:23], refs[23:]
    (
        x_ref,
        plane_taps,
        plane_bias,
        shift_taps,
        shift_bias,
        gain_ref,
        qkv_ref,
        exit_ref,
        scale_ref,
        gate_ref,
        gate_bias,
    ) = held
    (
        fields,
        slabs,
        lines,
        padded,
        second,
        joined,
        mixed,
        back,
        returned,
        stage,
        w_plane,
        w_shift,
        w_qkv,
        w_exit,
        w_gate,
        halo_send,
        halo_recv,
        there_send,
        there_recv,
        back_send,
        back_recv,
        load,
    ) = refs
    nr, nd, nc, H, W, bl, C, layers, taps, heads = sizes
    pack = LANES // C
    B = nd * bl
    half = taps // 2
    reach = (half + pack - 1) // pack
    hr = H // nd
    step = 8 if W % 8 == 0 else W
    parts = W // step
    seq = list(range(1, H - 1)) + sorted({0, H - 1})
    stages = [seq[a * nd : (a + 1) * nd] for a in range(hr)]
    row, disp, col = lax.axis_index("rows"), lax.axis_index("disp"), lax.axis_index("cols")

    def exists(dy, dx):
        ok = None
        for d, at, n in ((dy, row, nr), (dx, col, nc)):
            if d == -1:
                c = at > 0
            elif d == 1:
                c = at < n - 1
            else:
                continue
            ok = c if ok is None else jnp.logical_and(ok, c)
        return ok

    loads = [pltpu.make_async_copy(a, b, load.at[i]) for i, (a, b) in enumerate(zip(sources, held))]
    for c in loads:
        c.start()

    barrier = pltpu.get_barrier_semaphore()
    expected = jnp.int32(nd - 1)
    for dy, dx in DIRECTIONS:
        here = exists(dy, dx)
        expected = expected + here.astype(jnp.int32)

        @pl.when(here)
        def _():
            pl.semaphore_signal(
                barrier, inc=1, device_id={"rows": row + dy, "cols": col + dx}, device_id_type=MESH
            )

    for o in range(1, nd):
        pl.semaphore_signal(
            barrier, inc=1, device_id={"disp": lax.rem(disp + o, nd)}, device_id_type=MESH
        )

    loads[0].wait()
    for h in range(H):
        for b in range(bl):
            block = x_ref[h, :, b * LANES : (b + 1) * LANES].astype(F32)
            for s in range(2):
                stage[s, h * bl * W + b * W : h * bl * W + (b + 1) * W, :] = block[
                    :, s * 128 : (s + 1) * 128
                ]
    for h in range(H):
        for w in range(W):
            for s in range(2):
                fields[0, 1 + h, 1 + w, :, s * 128 : (s + 1) * 128] = stage[
                    s, pl.ds(h * bl * W + w, bl, stride=W), :
                ].astype(BF16)

    pl.semaphore_wait(barrier, expected)

    def span(d, n):
        return slice(1, n + 1) if d == 0 else (slice(1, 2) if d == -1 else slice(n, n + 1))

    def landing(d, n):
        return slice(1, n + 1) if d == 0 else (slice(n + 1, n + 2) if d == -1 else slice(0, 1))

    def halo_copy(k, i):
        dy, dx = DIRECTIONS[i]
        return pltpu.make_async_remote_copy(
            src_ref=fields.at[k, span(dy, H), span(dx, W)],
            dst_ref=fields.at[k, landing(dy, H), landing(dx, W)],
            send_sem=halo_send.at[k, i],
            recv_sem=halo_recv.at[k, i],
            device_id={"rows": row + dy, "cols": col + dx},
            device_id_type=MESH,
        )

    order = sorted(range(8), key=lambda i: DIRECTIONS[i][1] != 0)

    def halo_start(k, sides):
        for i in order:
            if DIRECTIONS[i][0] not in sides:
                continue

            @pl.when(exists(*DIRECTIONS[i]))
            def _():
                halo_copy(k, i).start()

    def halo_wait(k, which):
        for i in which:
            dy, dx = DIRECTIONS[i]

            @pl.when(exists(-dy, -dx))
            def _():
                halo_copy(k, i).wait_recv()

    halo_start(0, (-1, 0, 1))

    for i in range(8):
        dy, dx = DIRECTIONS[i]

        @pl.when(jnp.logical_not(exists(-dy, -dx)))
        def _():
            for k in range(layers):
                view = fields.at[k, landing(dy, H), landing(dx, W)]
                view[...] = jnp.zeros(view.shape, BF16)

    r_at = lax.broadcasted_iota(jnp.int32, (C, LANES), 0)
    l_at = lax.broadcasted_iota(jnp.int32, (C, LANES), 1)
    repeat = (l_at % C == r_at).astype(BF16)
    group = l_at // C

    def spread(w):
        return dot(w, repeat)

    for c in loads[1:]:
        c.wait()

    def plane_weights(l):
        for t in range(9):
            wide = spread(plane_taps[(l * 9 + t) * C : (l * 9 + t + 1) * C, :])
            for i in range(pack):
                at = t * LANES + i * C
                w_plane[l, at : at + C, :] = jnp.where(group == i, wide, 0.0).astype(BF16)

    bias_p = jnp.concatenate([plane_bias[...]] * pack, axis=1)
    bias_s = jnp.concatenate([shift_bias[...]] * pack, axis=1)
    bias_g = jnp.concatenate([gate_bias[...]] * pack, axis=1)
    gain = jnp.concatenate([gain_ref[...]] * pack, axis=1)

    def shift_weights(l):
        wides = [
            spread(shift_taps[(l * taps + t) * C : (l * taps + t + 1) * C, :]) for t in range(taps)
        ]
        for j in range(-reach, reach + 1):
            for i in range(pack):
                value = jnp.zeros((C, LANES), F32)
                for o in range(pack):
                    t = pack * j + i - o + half
                    if 0 <= t < taps:
                        value = jnp.where(group == o, wides[t], value)
                at = (j + reach) * LANES + i * C
                w_shift[l, at : at + C, :] = value.astype(BF16)

    def small_weights():
        a = lax.broadcasted_iota(jnp.int32, (3 * C, 3 * 128), 0)
        b = lax.broadcasted_iota(jnp.int32, (3 * C, 3 * 128), 1)
        place = jnp.logical_and(a // C == b // 128, a % C == b % 128).astype(BF16)
        wide = dot(qkv_ref[...], place).astype(BF16)
        w_qkv[...] = jnp.zeros(w_qkv.shape, BF16)
        for i in range(pack):
            w_qkv[i * C : (i + 1) * C, i * 384 : (i + 1) * 384] = wide
        w_exit[...] = jnp.zeros(w_exit.shape, BF16)
        wide = spread(exit_ref[...])
        for i in range(pack):
            w_exit[i * 128 : i * 128 + C, :] = jnp.where(group == i, wide, 0.0).astype(BF16)
        wide = spread(gate_ref[...])
        for i in range(pack):
            w_gate[i * C : (i + 1) * C, :] = jnp.where(group == i, wide, 0.0).astype(BF16)
        padded[:, 0:8, :] = jnp.zeros((W, 8, LANES), F32)
        padded[:, B + 8 : B + 16, :] = jnp.zeros((W, 8, LANES), F32)

    def there_copy(a, o):
        to = lax.rem(disp + o, nd)
        return pltpu.make_async_remote_copy(
            src_ref=slabs.at[a, to],
            dst_ref=lines.at[a, disp],
            send_sem=there_send.at[a, o - 1],
            recv_sem=there_recv.at[a, o - 1],
            device_id={"disp": to},
            device_id_type=MESH,
        )

    def plane_rows(k, h, n):
        lhs = jnp.concatenate(
            [
                fields[k, pl.ds(h + dy, n), dx : dx + W].reshape(n * W * bl, LANES)
                for dy in range(3)
                for dx in range(3)
            ],
            axis=1,
        )
        v = dot(lhs, w_plane[k]) + bias_p[k : k + 1]
        return (v * sigmoid(v)).astype(BF16).reshape(n, W, bl, LANES)

    def plane_row(k, h, slot=None, n=1):
        v = plane_rows(k, h, n)
        if k + 1 < layers:
            fields[k + 1, 1 + h : 1 + h + n, 1 : W + 1] = v
        else:
            slabs[slot] = v[0]

    sides = [i for i in range(8) if DIRECTIONS[i][0] == 0]
    below = [i for i in range(8) if DIRECTIONS[i][0] == -1]
    above = [i for i in range(8) if DIRECTIONS[i][0] == 1]
    plane_weights(0)
    for k in range(layers - 1):
        halo_wait(k, sides)
        if H > 2:
            plane_row(k, 1, n=H - 2)
        plane_weights(k + 1)
        if k == 0:
            small_weights()
        if k == layers - 2:
            shift_weights(0)
        halo_wait(k, above)
        if H > 1:
            plane_row(k, 0)
            halo_start(k + 1, (-1,))
        halo_wait(k, below)
        plane_row(k, H - 1)
        halo_start(k + 1, (1, 0) if H > 1 else (-1, 1, 0))

    k = layers - 1
    halo_wait(k, sides)
    waited = False
    for a, rows_here in enumerate(stages):
        inner = [h for h in rows_here if 0 < h < H - 1]
        outer = [h for h in rows_here if not 0 < h < H - 1]
        if outer and not inner and not waited:
            shift_weights(1)
            halo_wait(k, above + below)
            waited = True
        if len(inner) == nd == H - 2:
            v = plane_rows(k, 1, nd)
            for n in range(nd):
                slabs[a, n] = v[n]
            for o in range(1, nd):
                there_copy(a, o).start()
        elif len(inner) == nd or len(outer) == nd == 2:
            for o in list(range(1, nd)) + [0]:
                q = lax.rem(disp + o, nd)
                h = 1 + a * nd + q if inner else q * (H - 1)
                plane_row(k, h, (a, q))
                if o:
                    there_copy(a, o).start()
        else:
            for h in inner:
                plane_row(k, h, (a, rows_here.index(h)))
            if outer and not waited:
                shift_weights(1)
                halo_wait(k, above + below)
                waited = True
            for h in outer:
                plane_row(k, h, (a, rows_here.index(h)))
            for o in range(1, nd):
                there_copy(a, o).start()
        lines[a, disp] = slabs[a, disp]

    def shift_conv(l):
        lhs = jnp.concatenate(
            [
                padded[:, 8 + j : 8 + j + B, :].astype(BF16).reshape(W * B, LANES)
                for j in range(-reach, reach + 1)
            ],
            axis=1,
        )
        return dot(lhs, w_shift[l]) + bias_s[l : l + 1]

    ones_a = lax.broadcasted_iota(jnp.int32, (LANES, LANES), 0) // C
    ones_b = lax.broadcasted_iota(jnp.int32, (LANES, LANES), 1) // C
    ones = (ones_a == ones_b).astype(BF16)

    def conv_rows():
        v = shift_conv(0)
        v = (v * sigmoid(v)).astype(BF16).astype(F32)
        padded[:, 8 : 8 + B, :] = v.reshape(W, B, LANES)
        v = shift_conv(1).astype(BF16)
        second[...] = v.reshape(W, B, LANES)
        v = v.astype(F32)
        square = v * v
        high = square.astype(BF16)
        low = (square - high.astype(F32)).astype(BF16)
        mean = (dot(high, ones) + dot(low, ones)) * (1.0 / C)
        normed = (v * lax.rsqrt(mean + 1e-05) * gain).astype(BF16)
        joined[...] = dot(normed, w_qkv[...]).astype(BF16).reshape(W, B, pack * 384)

    D = pack * B
    hd = C // heads
    lane = lax.broadcasted_iota(jnp.int32, (D, 128), 1)
    together = LANES // D if heads % max(LANES // D, 1) == 0 else 1
    together = max(together, 1)
    factor = math.log2(math.e) / math.sqrt(hd)
    ones_rows = jnp.ones((16, D), BF16)
    scales = [
        jnp.concatenate(
            [
                jnp.broadcast_to(scale_ref[:, h : h + 1] * factor, (1, D))
                for h in range(g, g + together)
            ],
            axis=1,
        )
        for g in range(0, heads, together)
    ]

    def one_pixel(p):
        t = joined[p]
        q, k, v = (
            jnp.concatenate(
                [t[:, i * 384 + g * 128 : i * 384 + (g + 1) * 128] for i in range(pack)], axis=0
            )
            for g in range(3)
        )
        vt = v.astype(F32).T.astype(BF16)
        outs = []
        for n, g in enumerate(range(0, heads, together)):
            queries = jnp.concatenate(
                [
                    jnp.where(lane // hd == h, q, jnp.zeros_like(q))
                    for h in range(g, g + together)
                ],
                axis=0,
            )
            scores = lax.dot_general(
                k, queries, (((1,), (1,)), ((), ())), preferred_element_type=F32
            )
            top = jnp.max(scores, axis=0, keepdims=True)
            weights = jnp.exp2((scores - top) * scales[n]).astype(BF16)
            values = jnp.concatenate([vt[g * hd : (g + together) * hd], ones_rows], axis=0)
            o = dot(values, weights)
            inverse = 1.0 / o[together * hd : together * hd + 1]
            for i in range(together):
                cut = slice(i * D, (i + 1) * D)
                outs.append(o[i * hd : (i + 1) * hd, cut] * inverse[:, cut])
        o = jnp.concatenate(outs, axis=0)
        if C < 128:
            o = jnp.concatenate([o, jnp.zeros((128 - C, D), F32)], axis=0)
        o = o.T.astype(BF16)
        for i in range(pack):
            mixed[p, :, i * 128 : (i + 1) * 128] = o[i * B : (i + 1) * B]

    group_px = 8 if step % 8 == 0 else 1

    def back_copy(a, part, o):
        to = lax.rem(disp + o, nd)
        cut = pl.ds(part * step, step)
        return pltpu.make_async_remote_copy(
            src_ref=back.at[a, to, cut],
            dst_ref=returned.at[a, disp, cut],
            send_sem=back_send.at[a, part, o - 1],
            recv_sem=back_recv.at[a, part, o - 1],
            device_id={"disp": to},
            device_id_type=MESH,
        )

    def exit_chunk(a, p0):
        v = second[pl.ds(p0, step)].astype(F32).reshape(step * B, LANES)
        v = v + dot(mixed[pl.ds(p0, step)].reshape(step * B, pack * 128), w_exit[...])
        v = v.astype(BF16).reshape(step, B, LANES)
        for s in range(nd):
            back[a, s, pl.ds(p0, step)] = v[:, s * bl : (s + 1) * bl]
        returned[a, disp, pl.ds(p0, step)] = back[a, disp, pl.ds(p0, step)]

    for a in range(hr):
        for o in range(1, nd):
            there_copy(a, o).wait_recv()
        for s in range(nd):
            padded[:, 8 + s * bl : 8 + (s + 1) * bl, :] = lines[a, s].astype(F32)

        conv_rows()

        def one_part(part, carry):
            p0 = part * step

            def pixels(c, inner):
                for i in range(group_px):
                    one_pixel(p0 + c * group_px + i)
                return inner

            lax.fori_loop(0, step // group_px, pixels, 0)
            exit_chunk(a, p0)
            for o in range(1, nd):
                back_copy(a, part, o).start()
            return carry

        lax.fori_loop(0, parts, one_part, 0)

    for a, rows_here in enumerate(stages):
        for part in range(parts):
            for o in range(1, nd):
                back_copy(a, part, o).wait_recv()
            for n, h in enumerate(rows_here):
                w0 = part * step
                v = returned[a, n, w0 : w0 + step].reshape(step * bl, LANES)
                v = sigmoid(dot(v, w_gate[...]) + bias_g)
                at = (h * W + w0) * bl
                for s in range(2):
                    stage[s, at : at + step * bl, :] = v[:, s * 128 : (s + 1) * 128]
        for h in rows_here:
            for b in range(bl):
                for s in range(2):
                    out_ref[h, :, b * LANES + s * 128 : b * LANES + (s + 1) * 128] = stage[
                        s, pl.ds(h * W * bl + b, W, stride=bl), :
                    ]

    for k in range(layers):
        for i in range(8):
            @pl.when(exists(*DIRECTIONS[i]))
            def _():
                halo_copy(k, i).wait_send()
    for o in range(1, nd):
        for a in range(hr):
            there_copy(a, o).wait_send()
            for part in range(parts):
                back_copy(a, part, o).wait_send()


def per_device(axes, x, ptaps, pbias, staps, sbias, gain, qkv, wexit, scale, gate, gbias):
    nr, nd, nc = axes
    H, W, flat = x.shape
    C = ptaps.shape[-1]
    layers, taps, heads = ptaps.shape[0], staps.shape[1], scale.shape[0]
    pack = LANES // C
    bl = flat // LANES
    B = nd * bl
    hr = H // nd
    parts = W // 8 if W % 8 == 0 else 1
    reach = (taps // 2 + pack - 1) // pack
    sizes = (nr, nd, nc, H, W, bl, C, layers, taps, heads)
    peers = max(nd - 1, 1)
    arguments = (
        x,
        ptaps.reshape(-1, C),
        pbias,
        staps.reshape(-1, C),
        sbias,
        gain.reshape(1, C),
        qkv,
        wexit,
        scale.reshape(1, heads),
        gate,
        gbias.reshape(1, C),
    )
    gate = pl.pallas_call(
        functools.partial(kernel, sizes),
        out_shape=jax.ShapeDtypeStruct(x.shape, F32),
        in_specs=[pl.BlockSpec(memory_space=pltpu.HBM)] * len(arguments),
        out_specs=pl.BlockSpec(memory_space=pltpu.VMEM),
        scratch_shapes=[pltpu.VMEM(v.shape, v.dtype) for v in arguments]
        + [
            pltpu.VMEM((layers, H + 2, W + 2, bl, LANES), BF16),
            pltpu.VMEM((hr, nd, W, bl, LANES), BF16),
            pltpu.VMEM((hr, nd, W, bl, LANES), BF16),
            pltpu.VMEM((W, B + 16, LANES), F32),
            pltpu.VMEM((W, B, LANES), BF16),
            pltpu.VMEM((W, B, pack * 384), BF16),
            pltpu.VMEM((W, B, pack * 128), BF16),
            pltpu.VMEM((hr, nd, W, bl, LANES), BF16),
            pltpu.VMEM((hr, nd, W, bl, LANES), BF16),
            pltpu.VMEM((2, H * W * bl, 128), F32),
            pltpu.VMEM((layers, 9 * LANES, LANES), BF16),
            pltpu.VMEM((2, (2 * reach + 1) * LANES, LANES), BF16),
            pltpu.VMEM((LANES, pack * 384), BF16),
            pltpu.VMEM((pack * 128, LANES), BF16),
            pltpu.VMEM((LANES, LANES), BF16),
            pltpu.SemaphoreType.DMA((layers, 8)),
            pltpu.SemaphoreType.DMA((layers, 8)),
            pltpu.SemaphoreType.DMA((hr, peers)),
            pltpu.SemaphoreType.DMA((hr, peers)),
            pltpu.SemaphoreType.DMA((hr, parts, peers)),
            pltpu.SemaphoreType.DMA((hr, parts, peers)),
            pltpu.SemaphoreType.DMA((len(arguments),)),
        ],
        compiler_params=pltpu.CompilerParams(
            collective_id=0, has_side_effects=True, vmem_limit_bytes=63 * 1024 * 1024
        ),
    )(*arguments)
    return (x.astype(F32) * gate).astype(x.dtype)


def solution(mesh):
    axes = tuple(mesh.shape[a] for a in ("rows", "disp", "cols"))
    spec = P(("groups", "rows"), "cols", "disp")
    return jax.shard_map(
        functools.partial(per_device, axes),
        mesh=mesh,
        in_specs=(spec,) + (P(),) * 10,
        out_specs=spec,
        check_vma=False,
    )
```
